32 devices in a mesh: groups: 2 (over y), gx: 16 (over z, x, core).
Axes of the slice: x: 2, y: 2, z: 4, core: 2. Of those that a mesh axis runs over, the one named last changes fastest.
Arguments:
- hidden: bfloat16 [64, 8192], P('groups', 'gx'), parts along dimension 0, may hold values from -6 to 6
- norm_in_gain: float32 [8192], replicated, may hold values from 0.1 to 1.9
- w_z: bfloat16 [8192, 8192], P(None, 'gx'), may hold values from -0.0625 to 0.0625
- w_x: bfloat16 [8192, 8192], P(None, 'gx'), may hold values from -0.0625 to 0.0625
- w_dt: bfloat16 [8192, 128], P(None, 'gx'), may hold values from -0.0625 to 0.0625
- w_bc: bfloat16 [8192, 2048], P(None, 'gx'), may hold values from -0.0625 to 0.0625
- dt_bias: float32 [128], P('gx'), may hold values from -1 to 1
- decay_rate: float32 [128], P('gx'), may hold values from 0.2 to 4
- skip_gain: float32 [128], P('gx'), may hold values from 0.5 to 1.5
- conv_x_weight: float32 [4, 8192], P(None, 'gx'), may hold values from -3 to 3
- conv_bc_weight: float32 [4, 2048], P(None, 'gx'), may hold values from -3 to 3
- conv_x_state: bfloat16 [64, 3, 8192], P('groups', None, 'gx'), parts along dimension 0, may hold values from -6 to 6
- conv_bc_state: bfloat16 [64, 3, 2048], P('groups', None, 'gx'), parts along dimension 0, may hold values from -6 to 6
- ssm_state: float32 [64, 128, 64, 256], P('groups', 'gx'), parts along dimension 0, may hold values from -6 to 6
- group_gain: float32 [8192], P('gx'), may hold values from 0.1 to 1.9
- w_out: bfloat16 [8192, 8192], P('gx'), may hold values from -0.09375 to 0.09375
- norm_mid_gain: float32 [8192], replicated, may hold values from 0.1 to 1.9
- w_up: bfloat16 [8192, 16384], P(None, 'gx'), may hold values from -0.0625 to 0.0625
- w_down: bfloat16 [16384, 8192], P('gx'), may hold values from -0.0625 to 0.0625
Outputs:
- result: bfloat16 [64, 8192], P('groups', 'gx'), parts along dimension 0
- ssm_new: float32 [64, 128, 64, 256], P('groups', 'gx'), parts along dimension 0
- conv_x_new: bfloat16 [64, 3, 8192], P('groups', None, 'gx'), parts along dimension 0
- conv_bc_new: bfloat16 [64, 3, 2048], P('groups', None, 'gx'), parts along dimension 0
The draws below stay inside these ranges and needn't reach their ends.
There are 2 independent parts, one for each index of `groups`. The reference program is written for one: setup_inputs(seed, part) draws one part's arguments, and reference() takes and returns one part's arrays. A program takes and returns all parts, laid end to end along the dimension named above; an argument that names none is the same for every part. Nothing has to cross between parts.
All inputs are finite; a program needn't handle non-finite values.
Results may differ from the reference program's by a relative error of at most 0.0081.
Values may be sent and summed in bfloat16 or wider, within the bound.
A program may use at most 192 MiB of HBM per device.

```python
import math
import jax
import jax.numpy as jnp
from jax import lax

D = 8192
HEADS = 128
HEAD_DIM = 64
N = 256
G = 4
K = 4
FF = 16384
REQ = 32
INNER = 8192


def raised(values, rng, source, target, parts, factor):
    owner, partner = [(jnp.arange(values.shape[position]) // (values.shape[position] // parts)).reshape([-1 if axis == position else 1 for axis in range(values.ndim)]) for position in (source, target)]
    chosen = jax.random.permutation(rng, parts)[partner]
    strong = (owner == chosen) | (owner == (partner + parts // 2) % parts)
    return jnp.where(strong, factor * values, values)


def level_of(rng, shape, shards, least, top_value):
    gain, own = 1.0, jax.random.fold_in(rng, 6)
    for position, parts in shards:
        draws = jnp.exp(jax.random.uniform(jax.random.fold_in(own, position), (parts,), jnp.float32, least / len(shards), top_value / len(shards)))
        gain = gain * jnp.repeat(draws, shape[position] // parts).reshape([-1 if axis == position else 1 for axis in range(len(shape))])
    return gain


def gaussian(own_key, extent, scale, limit, split=(), held_as=jnp.bfloat16):
    factor_of = level_of(own_key, extent, split, -0.22, 0.18) if split else 1.0
    array = jax.random.normal(own_key, extent, jnp.float32) * scale * factor_of
    return jnp.minimum(jnp.maximum(array, -limit), limit).astype(held_as)


def gaussian_with(stream_key, shape, width, reach, split, heavy, kind=jnp.bfloat16):
    entries = width * jax.random.normal(stream_key, shape, jnp.float32)
    if split:
        entries = entries * level_of(stream_key, shape, split, -0.22, 0.18)
    return jnp.clip(raised(entries, jax.random.fold_in(stream_key, 3), *heavy), -reach, reach).astype(kind)


def setup_inputs(seed: int = 0, part: int = 0) -> dict:
    splits = jax.random.split(jax.random.key(seed), 20)
    part_splits = jax.random.split(jax.random.fold_in(splits[19], part), 20)
    hidden = gaussian(part_splits[0], (REQ, D), 1.0, 6.0, ((1, 16),))
    norm_in_gain = jnp.clip(1.0 + 0.18 * jax.random.normal(splits[1], (D,), jnp.float32), 0.1, 1.9)
    w_z = gaussian(splits[2], (D, INNER), D ** -0.5, 0.0625, ((1, 16),))
    w_x = gaussian(splits[3], (D, INNER), D ** -0.5, 0.0625, ((1, 16),))
    w_dt = gaussian(splits[4], (D, HEADS), D ** -0.5, 0.0625, ((1, 16),))
    w_bc = gaussian(splits[5], (D, 2 * G * N), D ** -0.5, 0.0625, ((1, 16),))
    dt_bias = jnp.clip(jax.random.uniform(splits[6], (HEADS,), jnp.float32, -1.0, 1.0) * level_of(splits[6], (HEADS,), ((0, 16),), -0.4, 0.0), -1.0, 1.0)
    decay_rate = jnp.clip(jnp.exp(math.log(4.0) - 2.9957323 * jax.random.uniform(splits[7], (HEADS,), jnp.float32) ** level_of(splits[7], (HEADS,), ((0, 16),), -0.2, 0.2)), 0.2, 4.0)
    skip_gain = jnp.clip(0.5 + 1.0 * jax.random.uniform(splits[8], (HEADS,), jnp.float32) ** level_of(splits[8], (HEADS,), ((0, 16),), -0.2, 0.2), 0.5, 1.5)
    conv_x_weight = gaussian(splits[9], (K, INNER), 0.5, 3.0, ((1, 16),), jnp.float32)
    conv_bc_weight = gaussian(splits[10], (K, 2 * G * N), 0.5, 3.0, ((1, 16),), jnp.float32)
    conv_x_state = gaussian(part_splits[11], (REQ, K - 1, INNER), 1.0, 6.0, ((2, 16),))
    conv_bc_state = gaussian(part_splits[12], (REQ, K - 1, 2 * G * N), 1.0, 6.0, ((2, 16),))
    ssm_state = gaussian(part_splits[13], (REQ, HEADS, HEAD_DIM, N), 1.0, 6.0, ((1, 16),), jnp.float32)
    group_gain = jnp.clip(1.0 + 0.18 * jax.random.normal(splits[14], (INNER,), jnp.float32), 0.1, 1.9)
    w_out = gaussian_with(splits[15], (INNER, D), INNER ** -0.5, 0.09375, ((0, 16),), (0, 1, 16, 2.0))
    norm_mid_gain = jnp.clip(1.0 + 0.18 * jax.random.normal(splits[16], (D,), jnp.float32), 0.1, 1.9)
    w_up = gaussian(splits[17], (D, FF), D ** -0.5, 0.0625, ((1, 16),))
    w_down = gaussian_with(splits[18], (FF, D), FF ** -0.5, 0.0625, ((0, 16),), (0, 1, 16, 2.0))
    return dict(hidden=hidden, norm_in_gain=norm_in_gain, w_z=w_z, w_x=w_x, w_dt=w_dt, w_bc=w_bc, dt_bias=dt_bias, decay_rate=decay_rate, skip_gain=skip_gain, conv_x_weight=conv_x_weight, conv_bc_weight=conv_bc_weight, conv_x_state=conv_x_state, conv_bc_state=conv_bc_state, ssm_state=ssm_state, group_gain=group_gain, w_out=w_out, norm_mid_gain=norm_mid_gain, w_up=w_up, w_down=w_down)


def rms_norm(values, gain_vec):
    inv_scale = lax.rsqrt(lax.optimization_barrier(jnp.mean(values * values, axis=-1, keepdims=True)) + 1e-05)
    return values * inv_scale * gain_vec

def conv_step(conv_state, fresh_cols, weight):
    window = jnp.concatenate([conv_state, fresh_cols[:, None, :]], axis=1)
    conv_sum = jnp.einsum('rkc,kc->rc', window.astype(jnp.float32), weight.astype(jnp.float32), precision=lax.Precision.HIGHEST)
    return (jax.nn.silu(conv_sum), window[:, 1:])

def reference(hidden, norm_in_gain, w_z, w_x, w_dt, w_bc, dt_bias, decay_rate, skip_gain, conv_x_weight, conv_bc_weight, conv_x_state, conv_bc_state, ssm_state, group_gain, w_out, norm_mid_gain, w_up, w_down):
    req_rows = hidden.shape[0]
    hidden_f = hidden.astype(jnp.float32)
    normed = rms_norm(hidden_f, norm_in_gain).astype(jnp.bfloat16)
    gate_z = jnp.dot(normed, w_z, preferred_element_type=jnp.float32)
    step_raw = jnp.dot(normed, w_dt, preferred_element_type=jnp.float32)
    x_raw = jnp.dot(normed, w_x, preferred_element_type=jnp.float32).astype(jnp.bfloat16)
    bc_raw = jnp.dot(normed, w_bc, preferred_element_type=jnp.float32).astype(jnp.bfloat16)
    x_conv, conv_x_new = conv_step(conv_x_state, x_raw, conv_x_weight)
    bc_conv, conv_bc_new = conv_step(conv_bc_state, bc_raw, conv_bc_weight)
    bc_vals = bc_conv.astype(jnp.bfloat16).astype(jnp.float32)
    b_heads = jnp.repeat(bc_vals[:, :G * N].reshape(req_rows, G, N), HEADS // G, axis=1)
    c_heads = jnp.repeat(bc_vals[:, G * N:].reshape(req_rows, G, N), HEADS // G, axis=1)
    step_size = jax.nn.softplus(step_raw + dt_bias)
    retain = jnp.exp(-step_size * decay_rate)
    x_heads = x_conv.reshape(req_rows, HEADS, HEAD_DIM)
    ssm_new = retain[:, :, None, None] * ssm_state + (step_size[:, :, None] * x_heads)[..., None] * b_heads[:, :, None, :]
    head_out = jnp.einsum('rhpn,rhn->rhp', ssm_new, c_heads, precision=lax.Precision.HIGHEST) + skip_gain[None, :, None] * x_heads
    gated_out = head_out.reshape(req_rows, INNER) * jax.nn.silu(gate_z)
    grouped = gated_out.reshape(req_rows, G, INNER // G)
    mean_sq = lax.optimization_barrier(jnp.mean(grouped * grouped, axis=-1, keepdims=True))
    y_normed = ((grouped * lax.rsqrt(mean_sq + 1e-05)).reshape(req_rows, INNER) * group_gain).astype(jnp.bfloat16)
    mixer_out = jnp.dot(y_normed, w_out, preferred_element_type=jnp.float32)
    after_mix = (hidden_f + mixer_out).astype(jnp.bfloat16)
    mid_normed = rms_norm(after_mix.astype(jnp.float32), norm_mid_gain).astype(jnp.bfloat16)
    hidden_up = jnp.dot(mid_normed, w_up, preferred_element_type=jnp.float32)
    active = jnp.square(jnp.maximum(hidden_up, 0.0)).astype(jnp.bfloat16)
    down_sum = jnp.dot(active, w_down, preferred_element_type=jnp.float32)
    result = (after_mix.astype(jnp.float32) + down_sum).astype(jnp.bfloat16)
    return (result, ssm_new, conv_x_new, conv_bc_new)
```

```python
import functools

import jax
import jax.numpy as jnp
from jax import lax
from jax.experimental import pallas as pl
from jax.experimental.pallas import tpu as pltpu
from jax.sharding import PartitionSpec as P

D = 8192
HEADS = 128
HEAD_DIM = 64
N = 256
G = 4
INNER = 8192


def rms_norm(values, gain_vec):
    inv_scale = lax.rsqrt(jnp.mean(values * values, axis=-1, keepdims=True) + 1e-05)
    return values * inv_scale * gain_vec


def conv_step(conv_state, fresh_cols, weight):
    window = jnp.concatenate([conv_state, fresh_cols[:, None, :]], axis=1)
    conv_sum = jnp.einsum(
        "rkc,kc->rc", window.astype(jnp.float32), weight, precision=lax.Precision.HIGHEST
    )
    return (jax.nn.silu(conv_sum), window[:, 1:])


def plain_body(
    hidden,
    norm_in_gain,
    w_z,
    w_x,
    w_dt,
    w_bc,
    dt_bias,
    decay_rate,
    skip_gain,
    conv_x_weight,
    conv_bc_weight,
    conv_x_state,
    conv_bc_state,
    ssm_state,
    group_gain,
    w_out,
    norm_mid_gain,
    w_up,
    w_down,
):
    position = lax.axis_index("gx")
    width_dev = hidden.shape[1]
    req_rows = hidden.shape[0]
    heads_dev = ssm_state.shape[1]
    full_rows = lax.all_gather(hidden, "gx", axis=1, tiled=True)
    normed = rms_norm(full_rows.astype(jnp.float32), norm_in_gain).astype(jnp.bfloat16)
    gate_z = jnp.dot(normed, w_z, preferred_element_type=jnp.float32)
    step_raw = jnp.dot(normed, w_dt, preferred_element_type=jnp.float32)
    x_raw = jnp.dot(normed, w_x, preferred_element_type=jnp.float32).astype(jnp.bfloat16)
    bc_raw = jnp.dot(normed, w_bc, preferred_element_type=jnp.float32).astype(jnp.bfloat16)
    x_conv, conv_x_new = conv_step(conv_x_state, x_raw, conv_x_weight)
    bc_conv, conv_bc_new = conv_step(conv_bc_state, bc_raw, conv_bc_weight)
    bc_full = lax.all_gather(bc_conv.astype(jnp.bfloat16), "gx", axis=1, tiled=True).astype(
        jnp.float32
    )
    group_idx = position * heads_dev // (HEADS // G)
    b_part = lax.dynamic_slice_in_dim(bc_full, group_idx * N, N, 1)
    c_part = lax.dynamic_slice_in_dim(bc_full, (G + group_idx) * N, N, 1)
    step_size = jax.nn.softplus(step_raw + dt_bias)
    retain = jnp.exp(-step_size * decay_rate)
    x_heads = x_conv.reshape(req_rows, heads_dev, HEAD_DIM)
    ssm_new = (
        retain[:, :, None, None] * ssm_state
        + (step_size[:, :, None] * x_heads)[..., None] * b_part[:, None, None, :]
    )
    head_out = (
        jnp.einsum("rhpn,rn->rhp", ssm_new, c_part, precision=lax.Precision.HIGHEST)
        + skip_gain[None, :, None] * x_heads
    )
    gated_out = head_out.reshape(req_rows, heads_dev * HEAD_DIM) * jax.nn.silu(gate_z)
    onehot = (jnp.arange(G) == group_idx).astype(jnp.float32)
    own_sq = jnp.sum(gated_out * gated_out, axis=-1)
    totals = lax.psum(own_sq[:, None] * onehot[None, :], "gx")
    mean_sq = jnp.sum(totals * onehot[None, :], axis=-1, keepdims=True) / (INNER // G)
    y_normed = (gated_out * lax.rsqrt(mean_sq + 1e-05) * group_gain).astype(jnp.bfloat16)
    mixer_terms = jnp.dot(y_normed, w_out, preferred_element_type=jnp.float32)
    mixer_out = lax.psum_scatter(mixer_terms, "gx", scatter_dimension=1, tiled=True)
    after_mix = (hidden.astype(jnp.float32) + mixer_out).astype(jnp.bfloat16)
    after_f = after_mix.astype(jnp.float32)
    total_sq = lax.psum(jnp.sum(after_f * after_f, axis=-1), "gx")
    gain_own = lax.dynamic_slice_in_dim(norm_mid_gain, position * width_dev, width_dev, 0)
    mid_own = (after_f * lax.rsqrt(total_sq[:, None] / D + 1e-05) * gain_own).astype(jnp.bfloat16)
    hidden_up = jnp.dot(
        lax.all_gather(mid_own, "gx", axis=1, tiled=True), w_up, preferred_element_type=jnp.float32
    )
    active = jnp.square(jnp.maximum(hidden_up, 0.0)).astype(jnp.bfloat16)
    down_sum = lax.psum_scatter(
        jnp.dot(active, w_down, preferred_element_type=jnp.float32),
        "gx",
        scatter_dimension=1,
        tiled=True,
    )
    result = (after_mix.astype(jnp.float32) + down_sum).astype(jnp.bfloat16)
    return (result, ssm_new, conv_x_new, conv_bc_new)


MESH = pl.DeviceIdType.MESH
NDEV = 16
LINES = 4
F32 = jnp.float32
BF16 = jnp.bfloat16
VM = pl.BlockSpec(memory_space=pltpu.VMEM)
HB = pl.BlockSpec(memory_space=pl.ANY)


def spot(z, x, c):
    return z * 4 + x * 2 + c


def coords():
    me = lax.axis_index("gx")
    return me, me // 4, (me // 2) % 2, me % 2


def remote(src, dst, send, recv, dev):
    return pltpu.make_async_remote_copy(
        src_ref=src, dst_ref=dst, send_sem=send, recv_sem=recv,
        device_id={"gx": dev}, device_id_type=MESH,
    )


def greet(me):
    barrier = pltpu.get_barrier_semaphore()
    for i in range(1, NDEV):
        pl.semaphore_signal(
            barrier, inc=1, device_id={"gx": (me + i) % NDEV}, device_id_type=MESH
        )
    pl.semaphore_wait(barrier, NDEV - 1)


def gather_blocks(blocks, send, recv):
    me, z, x, c = coords()
    started = []

    def put(b, dev):
        cp = remote(blocks.at[b], blocks.at[b], send.at[len(started)], recv.at[b], dev)
        cp.start()
        started.append(cp)

    def arrive(b):
        remote(blocks.at[b], blocks.at[b], send.at[0], recv.at[b], (me + 1) % NDEV).wait_recv()

    across, beside = spot(z, 1 - x, c), spot(z, x, 1 - c)
    for dz in (2, 1, 3):
        put(me, spot((z + dz) % LINES, x, c))
    put(me, across)
    put(me, beside)
    for dz in (1, 3, 2):
        b = spot((z + dz) % LINES, x, c)
        arrive(b)
        put(b, across)
        put(b, beside)
    for dz in (0, 1, 3, 2):
        b = spot((z + dz) % LINES, 1 - x, c)
        arrive(b)
        put(b, beside)
    for dz in (0, 1, 3, 2):
        arrive(spot((z + dz) % LINES, x, 1 - c))
        arrive(spot((z + dz) % LINES, 1 - x, 1 - c))
    return started


def norm_blocks(blocks, gain_ref, out):
    width = blocks.shape[2]
    total = jnp.zeros(blocks.shape[1:], F32)
    for k in range(NDEV):
        v = blocks[k].astype(F32)
        total += v * v
    inv = lax.rsqrt(jnp.sum(total, axis=1, keepdims=True) / (NDEV * width) + 1e-05)
    for k in range(NDEV):
        out[k] = (blocks[k].astype(F32) * inv * gain_ref[:, k * width : (k + 1) * width]).astype(BF16)


def spread_sum(part_fn, scale_fn, parts, csend, crecv, xsend, xrecv, zsend, zrecv, sems):
    me, z, x, c = coords()
    across, beside = spot(z, 1 - x, c), spot(z, x, 1 - c)
    cs, cr, xs, xr, zs, zr = sems
    ccp, xcp, zcp = {}, {}, {}
    own = None
    for step in range(LINES + 2):
        t = step
        if t < LINES:
            part_fn(t, parts)
            for xx in range(2):
                csend[t, xx] = parts[t, xx * 2 + (1 - c)].astype(BF16)
            ccp[t] = remote(csend.at[t], crecv.at[t], cs.at[t], cr.at[t], beside)
            ccp[t].start()
        t = step - 1
        if 0 <= t < LINES:
            ccp[t].wait_recv()
            xsend[t] = (parts[t, (1 - x) * 2 + c] + crecv[t, 1 - x].astype(F32)).astype(BF16)
            xcp[t] = remote(xsend.at[t], xrecv.at[t], xs.at[t], xr.at[t], across)
            xcp[t].start()
        t = step - 2
        if 0 <= t < LINES:
            xcp[t].wait_recv()
            v = parts[t, x * 2 + c] + crecv[t, x].astype(F32) + xrecv[t].astype(F32)
            v = scale_fn(v)
            if t < LINES - 1:
                zsend[t] = v.astype(BF16)
                zcp[t] = remote(
                    zsend.at[t], zrecv.at[t], zs.at[t], zr.at[t], spot((z + 1 + t) % LINES, x, c)
                )
                zcp[t].start()
            else:
                own = v
    for t in range(LINES - 1):
        zcp[t].wait_recv()
        own = own + zrecv[t].astype(F32)
    return own, list(ccp.values()) + list(xcp.values()) + list(zcp.values())


def conv_rows(state_ref, fresh, weight_ref, new_ref):
    total = fresh.astype(F32) * weight_ref[3:4, :]
    for k in range(3):
        total += state_ref[k].astype(F32) * weight_ref[k : k + 1, :]
    new_ref[0] = state_ref[1]
    new_ref[1] = state_ref[2]
    new_ref[2] = fresh
    return total / (1.0 + jnp.exp(-total))


def front_kernel(
    hid, gain, wz, wx, wbc, wdt, dtb, dec, cxw, cbw, cxs, cbs,
    xconv, gate, step, retain, bc, cxn, cbn,
    blocks, xn, wz_v, wx_v, wbc_v, bc_own, bc_got,
    wsem, bsem, ag_s, ag_r, bc_s, bc_r,
):
    me, z, x, c = coords()
    rows = wx_v.shape[1]
    bc_cp = pltpu.make_async_copy(wbc, wbc_v, bsem)
    bc_cp.start()
    loads = []
    for i, (src, dst) in enumerate(((wx, wx_v), (wz, wz_v))):
        for k in range(4):
            cp = pltpu.make_async_copy(
                src.at[pl.ds(k * rows, rows), :], dst.at[k], wsem.at[i * 4 + k]
            )
            cp.start()
            loads.append(cp)
    blocks[me] = hid[...]
    greet(me)
    started = gather_blocks(blocks, ag_s, ag_r)
    norm_blocks(blocks, gain, xn)
    width = hid.shape[1]

    bc_cp.wait()
    acc = jnp.zeros(bc_own.shape, F32)
    for k in range(NDEV):
        acc += jnp.dot(xn[k], wbc_v[k * width : (k + 1) * width, :], preferred_element_type=F32)
    bc_own[...] = conv_rows(cbs, acc.astype(BF16), cbw, cbn).astype(BF16)
    goal, slot = (me % 8) // 2, (me // 8) * 2 + me % 2
    for i in range(4):
        dev = goal * 4 + i

        @pl.when(dev != me)
        def _():
            remote(bc_own, bc_got.at[slot], bc_s.at[i], bc_r.at[slot], dev).start()

        @pl.when(dev == me)
        def _():
            bc_got[slot] = bc_own[...]

    def project(w_v, first):
        acc = jnp.zeros(xconv.shape, F32)
        for k in range(4):
            loads[first + k].wait()
            for j in range(4):
                acc += jnp.dot(
                    xn[k * 4 + j], w_v[k, j * width : (j + 1) * width, :],
                    preferred_element_type=F32,
                )
        return acc

    acc = jnp.zeros(step.shape, F32)
    for k in range(NDEV):
        acc += lax.dot_general(
            xn[k], wdt[:, k * width : (k + 1) * width], (((1,), (1,)), ((), ())),
            preferred_element_type=F32,
        )
    raw = acc + dtb[...]
    size = jnp.maximum(raw, 0.0) + jnp.log1p(jnp.exp(-jnp.abs(raw)))
    step[...] = size
    retain[...] = jnp.exp(-size * dec[...])
    xconv[...] = conv_rows(cxs, project(wx_v, 0).astype(BF16), cxw, cxn)
    zv = project(wz_v, 4)
    gate[...] = zv / (1.0 + jnp.exp(-zv))

    for i in range(4):
        src = (i // 2) * 8 + z * 2 + i % 2

        @pl.when(src != me)
        def _():
            remote(bc_own, bc_got.at[i], bc_s.at[0], bc_r.at[i], src).wait_recv()

    bc[...] = bc_got[...]
    for i in range(4):
        dev = goal * 4 + i

        @pl.when(dev != me)
        def _():
            remote(bc_own, bc_got.at[slot], bc_s.at[i], bc_r.at[slot], dev).wait_send()

    for cp in started:
        cp.wait_send()


def back_kernel(
    gated, ggain, hid, mgain, wo, wu, wd,
    result,
    wo_v, wu_v, wd_v, y, act, parts, blocks, xn, sq_own, sq_got,
    csend, crecv, xsend, xrecv, zsend, zrecv,
    wsem, sq_s, sq_r, ag_s, ag_r, rs1, rs2,
):
    me, z, x, c = coords()
    cols = wo_v.shape[2]
    rows = wu_v.shape[1]
    width = hid.shape[1]
    loads = {}
    for t in range(LINES):
        at = pl.multiple_of(((z + 1 + t) % LINES) * cols, cols)
        loads["o", t] = pltpu.make_async_copy(wo.at[:, pl.ds(at, cols)], wo_v.at[t], wsem.at[t])
    for t in range(LINES):
        loads["u", t] = pltpu.make_async_copy(
            wu.at[pl.ds(t * rows, rows), :], wu_v.at[t], wsem.at[4 + t]
        )
    for t in range(LINES):
        at = pl.multiple_of(((z + 1 + t) % LINES) * cols, cols)
        loads["d", t] = pltpu.make_async_copy(wd.at[:, pl.ds(at, cols)], wd_v.at[t], wsem.at[8 + t])
    for cp in loads.values():
        cp.start()
    g = gated[...]
    y[...] = (g * ggain[...]).astype(BF16)
    sq_own[...] = jnp.broadcast_to(jnp.sum(g * g, axis=1, keepdims=True), sq_own.shape)
    greet(me)
    mates = (spot(z, x, 1 - c), spot(z, 1 - x, c), spot(z, 1 - x, 1 - c))
    sq_cp = [remote(sq_own, sq_got.at[i], sq_s.at[i], sq_r.at[i], mates[i]) for i in range(3)]
    for cp in sq_cp:
        cp.start()
    scale = []

    def group_scale(v):
        if not scale:
            total = sq_own[...]
            for i in range(3):
                sq_cp[i].wait_recv()
                total = total + sq_got[i]
            scale.append(lax.rsqrt(total[:, :1] / (4 * width) + 1e-05))
        return v * scale[0]

    def part(name, lhs, w_v):
        def fn(t, out):
            loads[name, t].wait()
            for b in range(4):
                out[t, b] = jnp.dot(
                    lhs[...], w_v[t, :, b * width : (b + 1) * width], preferred_element_type=F32
                )
        return fn

    mix, started = spread_sum(
        part("o", y, wo_v), group_scale, parts,
        csend.at[0], crecv.at[0], xsend.at[0], xrecv.at[0], zsend.at[0], zrecv.at[0],
        [rs1.at[i] for i in range(6)],
    )
    after = (hid[...].astype(F32) + mix).astype(BF16)
    blocks[me] = after
    started += sq_cp + gather_blocks(blocks, ag_s, ag_r)
    norm_blocks(blocks, mgain, xn)
    acc = jnp.zeros(act.shape, F32)
    for t in range(LINES):
        loads["u", t].wait()
        for j in range(4):
            acc += jnp.dot(
                xn[t * 4 + j], wu_v[t, j * width : (j + 1) * width, :], preferred_element_type=F32
            )
    act[...] = jnp.square(jnp.maximum(acc, 0.0)).astype(BF16)
    down, more = spread_sum(
        part("d", act, wd_v), lambda v: v, parts,
        csend.at[1], crecv.at[1], xsend.at[1], xrecv.at[1], zsend.at[1], zrecv.at[1],
        [rs2.at[i] for i in range(6)],
    )
    result[...] = (blocks[me].astype(F32) + down).astype(BF16)
    for cp in started + more:
        cp.wait_send()


def body(
    hidden, norm_in_gain, w_z, w_x, w_dt, w_bc, dt_bias, decay_rate, skip_gain,
    conv_x_weight, conv_bc_weight, conv_x_state, conv_bc_state, ssm_state,
    group_gain, w_out, norm_mid_gain, w_up, w_down,
):
    req, width = hidden.shape
    dim = w_x.shape[0]
    heads_dev = ssm_state.shape[1]
    inner = w_x.shape[1]
    bcw = w_bc.shape[1]
    ff = w_up.shape[1]
    dma = pltpu.SemaphoreType.DMA
    xconv, gate, step, retain, bc, cxn, cbn = pl.pallas_call(
        front_kernel,
        out_shape=[
            jax.ShapeDtypeStruct((req, inner), F32),
            jax.ShapeDtypeStruct((req, inner), F32),
            jax.ShapeDtypeStruct((req, heads_dev), F32),
            jax.ShapeDtypeStruct((req, heads_dev), F32),
            jax.ShapeDtypeStruct((4, req, bcw), BF16),
            jax.ShapeDtypeStruct((3, req, inner), BF16),
            jax.ShapeDtypeStruct((3, req, bcw), BF16),
        ],
        in_specs=[VM, VM, HB, HB, HB] + [VM] * 7,
        out_specs=[VM] * 7,
        scratch_shapes=[
            pltpu.VMEM((NDEV, req, width), BF16),
            pltpu.VMEM((NDEV, req, width), BF16),
            pltpu.VMEM((4, dim // 4, inner), BF16),
            pltpu.VMEM((4, dim // 4, inner), BF16),
            pltpu.VMEM((dim, bcw), BF16),
            pltpu.VMEM((req, bcw), BF16),
            pltpu.VMEM((4, req, bcw), BF16),
            dma((8,)), dma, dma((15,)), dma((16,)), dma((4,)), dma((4,)),
        ],
        compiler_params=pltpu.CompilerParams(
            collective_id=0, has_side_effects=True, vmem_limit_bytes=32 << 20
        ),
        name="front",
    )(
        hidden, norm_in_gain[None], w_z, w_x, w_bc, w_dt.T, dt_bias[None], decay_rate[None],
        conv_x_weight, conv_bc_weight,
        conv_x_state.transpose(1, 0, 2), conv_bc_state.transpose(1, 0, 2),
    )
    b_part = jnp.concatenate([bc[0], bc[1]], axis=1).astype(F32)
    c_part = jnp.concatenate([bc[2], bc[3]], axis=1).astype(F32)
    x_heads = xconv.reshape(req, heads_dev, HEAD_DIM)
    ssm_new = (
        retain[:, :, None, None] * ssm_state
        + (step[:, :, None] * x_heads)[..., None] * b_part[:, None, None, :]
    )
    head_out = (
        jnp.einsum("rhpn,rn->rhp", ssm_new, c_part, precision=lax.Precision.HIGHEST)
        + skip_gain[None, :, None] * x_heads
    )
    gated = head_out.reshape(req, inner) * gate
    slot = (LINES, req, width)
    result = pl.pallas_call(
        back_kernel,
        out_shape=jax.ShapeDtypeStruct((req, width), BF16),
        in_specs=[VM] * 4 + [HB] * 3,
        out_specs=VM,
        scratch_shapes=[
            pltpu.VMEM((4, inner, dim // 4), BF16),
            pltpu.VMEM((4, dim // 4, ff), BF16),
            pltpu.VMEM((4, ff, dim // 4), BF16),
            pltpu.VMEM((req, inner), BF16),
            pltpu.VMEM((req, ff), BF16),
            pltpu.VMEM((4, 4, req, width), F32),
            pltpu.VMEM((NDEV, req, width), BF16),
            pltpu.VMEM((NDEV, req, width), BF16),
            pltpu.VMEM((req, 128), F32),
            pltpu.VMEM((3, req, 128), F32),
            pltpu.VMEM((2, 4, 2, req, width), BF16),
            pltpu.VMEM((2, 4, 2, req, width), BF16),
            pltpu.VMEM((2,) + slot, BF16),
            pltpu.VMEM((2,) + slot, BF16),
            pltpu.VMEM((2,) + slot, BF16),
            pltpu.VMEM((2,) + slot, BF16),
            dma((12,)), dma((3,)), dma((3,)), dma((15,)), dma((16,)), dma((6, 4)), dma((6, 4)),
        ],
        compiler_params=pltpu.CompilerParams(
            collective_id=1, has_side_effects=True, vmem_limit_bytes=52 << 20
        ),
        name="back",
    )(gated, group_gain[None], hidden, norm_mid_gain[None], w_out, w_up, w_down)
    return (result, ssm_new, cxn.transpose(1, 0, 2), cbn.transpose(1, 0, 2))


def solution(mesh):
    in_specs = (
        P("groups", "gx"),
        P(),
        P(None, "gx"),
        P(None, "gx"),
        P(None, "gx"),
        P(None, "gx"),
        P("gx"),
        P("gx"),
        P("gx"),
        P(None, "gx"),
        P(None, "gx"),
        P("groups", None, "gx"),
        P("groups", None, "gx"),
        P("groups", "gx", None, None),
        P("gx"),
        P("gx", None),
        P(),
        P(None, "gx"),
        P("gx", None),
    )
    out_specs = (
        P("groups", "gx"),
        P("groups", "gx", None, None),
        P("groups", None, "gx"),
        P("groups", None, "gx"),
    )
    chosen = body if mesh.shape["gx"] == NDEV else plain_body
    return jax.shard_map(chosen, mesh=mesh, in_specs=in_specs, out_specs=out_specs, check_vma=False)
```

```python
import functools

import jax
import jax.numpy as jnp
from jax import lax
from jax.experimental import pallas as pl
from jax.experimental.pallas import tpu as pltpu
from jax.sharding import PartitionSpec as P

D = 8192
HEADS = 128
HEAD_DIM = 64
N = 256
G = 4
INNER = 8192


def rms_norm(values, gain_vec):
    inv_scale = lax.rsqrt(jnp.mean(values * values, axis=-1, keepdims=True) + 1e-05)
    return values * inv_scale * gain_vec


def conv_step(conv_state, fresh_cols, weight):
    window = jnp.concatenate([conv_state, fresh_cols[:, None, :]], axis=1)
    conv_sum = jnp.einsum(
        "rkc,kc->rc", window.astype(jnp.float32), weight, precision=lax.Precision.HIGHEST
    )
    return (jax.nn.silu(conv_sum), window[:, 1:])


def plain_body(
    hidden,
    norm_in_gain,
    w_z,
    w_x,
    w_dt,
    w_bc,
    dt_bias,
    decay_rate,
    skip_gain,
    conv_x_weight,
    conv_bc_weight,
    conv_x_state,
    conv_bc_state,
    ssm_state,
    group_gain,
    w_out,
    norm_mid_gain,
    w_up,
    w_down,
):
    position = lax.axis_index("gx")
    width_dev = hidden.shape[1]
    req_rows = hidden.shape[0]
    heads_dev = ssm_state.shape[1]
    full_rows = lax.all_gather(hidden, "gx", axis=1, tiled=True)
    normed = rms_norm(full_rows.astype(jnp.float32), norm_in_gain).astype(jnp.bfloat16)
    gate_z = jnp.dot(normed, w_z, preferred_element_type=jnp.float32)
    step_raw = jnp.dot(normed, w_dt, preferred_element_type=jnp.float32)
    x_raw = jnp.dot(normed, w_x, preferred_element_type=jnp.float32).astype(jnp.bfloat16)
    bc_raw = jnp.dot(normed, w_bc, preferred_element_type=jnp.float32).astype(jnp.bfloat16)
    x_conv, conv_x_new = conv_step(conv_x_state, x_raw, conv_x_weight)
    bc_conv, conv_bc_new = conv_step(conv_bc_state, bc_raw, conv_bc_weight)
    bc_full = lax.all_gather(bc_conv.astype(jnp.bfloat16), "gx", axis=1, tiled=True).astype(
        jnp.float32
    )
    group_idx = position * heads_dev // (HEADS // G)
    b_part = lax.dynamic_slice_in_dim(bc_full, group_idx * N, N, 1)
    c_part = lax.dynamic_slice_in_dim(bc_full, (G + group_idx) * N, N, 1)
    step_size = jax.nn.softplus(step_raw + dt_bias)
    retain = jnp.exp(-step_size * decay_rate)
    x_heads = x_conv.reshape(req_rows, heads_dev, HEAD_DIM)
    ssm_new = (
        retain[:, :, None, None] * ssm_state
        + (step_size[:, :, None] * x_heads)[..., None] * b_part[:, None, None, :]
    )
    head_out = (
        jnp.einsum("rhpn,rn->rhp", ssm_new, c_part, precision=lax.Precision.HIGHEST)
        + skip_gain[None, :, None] * x_heads
    )
    gated_out = head_out.reshape(req_rows, heads_dev * HEAD_DIM) * jax.nn.silu(gate_z)
    onehot = (jnp.arange(G) == group_idx).astype(jnp.float32)
    own_sq = jnp.sum(gated_out * gated_out, axis=-1)
    totals = lax.psum(own_sq[:, None] * onehot[None, :], "gx")
    mean_sq = jnp.sum(totals * onehot[None, :], axis=-1, keepdims=True) / (INNER // G)
    y_normed = (gated_out * lax.rsqrt(mean_sq + 1e-05) * group_gain).astype(jnp.bfloat16)
    mixer_terms = jnp.dot(y_normed, w_out, preferred_element_type=jnp.float32)
    mixer_out = lax.psum_scatter(mixer_terms, "gx", scatter_dimension=1, tiled=True)
    after_mix = (hidden.astype(jnp.float32) + mixer_out).astype(jnp.bfloat16)
    after_f = after_mix.astype(jnp.float32)
    total_sq = lax.psum(jnp.sum(after_f * after_f, axis=-1), "gx")
    gain_own = lax.dynamic_slice_in_dim(norm_mid_gain, position * width_dev, width_dev, 0)
    mid_own = (after_f * lax.rsqrt(total_sq[:, None] / D + 1e-05) * gain_own).astype(jnp.bfloat16)
    hidden_up = jnp.dot(
        lax.all_gather(mid_own, "gx", axis=1, tiled=True), w_up, preferred_element_type=jnp.float32
    )
    active = jnp.square(jnp.maximum(hidden_up, 0.0)).astype(jnp.bfloat16)
    down_sum = lax.psum_scatter(
        jnp.dot(active, w_down, preferred_element_type=jnp.float32),
        "gx",
        scatter_dimension=1,
        tiled=True,
    )
    result = (after_mix.astype(jnp.float32) + down_sum).astype(jnp.bfloat16)
    return (result, ssm_new, conv_x_new, conv_bc_new)


MESH = pl.DeviceIdType.MESH
NDEV = 16
LINES = 4
F32 = jnp.float32
BF16 = jnp.bfloat16
VM = pl.BlockSpec(memory_space=pltpu.VMEM)
HB = pl.BlockSpec(memory_space=pltpu.HBM)


def spot(z, x, c):
    return z * 4 + x * 2 + c


def coords():
    me = lax.axis_index("gx")
    return me, me // 4, (me // 2) % 2, me % 2


def remote(src, dst, send, recv, dev):
    return pltpu.make_async_remote_copy(
        src_ref=src, dst_ref=dst, send_sem=send, recv_sem=recv,
        device_id={"gx": dev}, device_id_type=MESH,
    )


def greet(me):
    barrier = pltpu.get_barrier_semaphore()
    for i in range(1, NDEV):
        pl.semaphore_signal(
            barrier, inc=1, device_id={"gx": (me + i) % NDEV}, device_id_type=MESH
        )
    pl.semaphore_wait(barrier, NDEV - 1)


def gather_blocks(blocks, send, recv):
    me, z, x, c = coords()
    started = []

    def put(b, dev):
        cp = remote(blocks.at[b], blocks.at[b], send.at[len(started)], recv.at[b], dev)
        cp.start()
        started.append(cp)

    def arrive(b):
        remote(blocks.at[b], blocks.at[b], send.at[0], recv.at[b], (me + 1) % NDEV).wait_recv()

    across, beside = spot(z, 1 - x, c), spot(z, x, 1 - c)
    for dz in (2, 1, 3):
        put(me, spot((z + dz) % LINES, x, c))
    put(me, across)
    put(me, beside)
    for dz in (1, 3, 2):
        b = spot((z + dz) % LINES, x, c)
        arrive(b)
        put(b, across)
        put(b, beside)
    for dz in (0, 1, 3, 2):
        b = spot((z + dz) % LINES, 1 - x, c)
        arrive(b)
        put(b, beside)
    for dz in (0, 1, 3, 2):
        arrive(spot((z + dz) % LINES, x, 1 - c))
        arrive(spot((z + dz) % LINES, 1 - x, 1 - c))
    return started


def norm_blocks(blocks, gain_ref, out):
    width = blocks.shape[2]
    total = jnp.zeros(blocks.shape[1:], F32)
    for k in range(NDEV):
        v = blocks[k].astype(F32)
        total += v * v
    inv = lax.rsqrt(jnp.sum(total, axis=1, keepdims=True) / (NDEV * width) + 1e-05)
    for k in range(NDEV):
        out[k] = (blocks[k].astype(F32) * inv * gain_ref[:, k * width : (k + 1) * width]).astype(BF16)


def spread_sum(part_fn, scale_fn, parts, csend, crecv, xsend, xrecv, zsend, zrecv, sems):
    me, z, x, c = coords()
    across, beside = spot(z, 1 - x, c), spot(z, x, 1 - c)
    cs, cr, xs, xr, zs, zr = sems
    ccp, xcp, zcp = {}, {}, {}
    own = None
    for step in range(LINES + 2):
        t = step
        if t < LINES:
            part_fn(t, parts)
            for xx in range(2):
                csend[t, xx] = parts[t, xx * 2 + (1 - c)].astype(BF16)
            ccp[t] = remote(csend.at[t], crecv.at[t], cs.at[t], cr.at[t], beside)
            ccp[t].start()
        t = step - 1
        if 0 <= t < LINES:
            ccp[t].wait_recv()
            xsend[t] = (parts[t, (1 - x) * 2 + c] + crecv[t, 1 - x].astype(F32)).astype(BF16)
            xcp[t] = remote(xsend.at[t], xrecv.at[t], xs.at[t], xr.at[t], across)
            xcp[t].start()
        t = step - 2
        if 0 <= t < LINES:
            xcp[t].wait_recv()
            v = parts[t, x * 2 + c] + crecv[t, x].astype(F32) + xrecv[t].astype(F32)
            v = scale_fn(v)
            if t < LINES - 1:
                zsend[t] = v.astype(BF16)
                zcp[t] = remote(
                    zsend.at[t], zrecv.at[t], zs.at[t], zr.at[t], spot((z + 1 + t) % LINES, x, c)
                )
                zcp[t].start()
            else:
                own = v
    for t in range(LINES - 1):
        zcp[t].wait_recv()
        own = own + zrecv[t].astype(F32)
    return own, list(ccp.values()) + list(xcp.values()) + list(zcp.values())


def conv_rows(state_ref, fresh, weight_ref, new_ref):
    total = fresh.astype(F32) * weight_ref[3:4, :]
    for k in range(3):
        total += state_ref[k].astype(F32) * weight_ref[k : k + 1, :]
    new_ref[0] = state_ref[1]
    new_ref[1] = state_ref[2]
    new_ref[2] = fresh
    return total / (1.0 + jnp.exp(-total))


def per_channel(heads, shape):
    count = heads.shape[1]
    head = lax.broadcasted_iota(jnp.int32, shape, 1) // (shape[1] // count)
    out = jnp.zeros(shape, F32)
    for h in range(count):
        out = jnp.where(head == h, heads[:, h : h + 1], out)
    return out


def state_kernel(
    state, sizex, retain, skipx, gate, bc, cx, cb,
    new_state, gated, cx_out, cb_out,
):
    @pl.when((pl.program_id(0) == 0) & (pl.program_id(1) == 0))
    def _():
        cx_out[...] = cx[...]
        cb_out[...] = cb[...]

    reqs, heads, chans, _ = state.shape
    wide = heads * chans
    copies = wide // reqs
    sx = jnp.concatenate([sizex[...]] * copies, axis=0).T
    rt = jnp.concatenate([retain[...]] * copies, axis=0).T
    first = pl.multiple_of(pl.program_id(0) * reqs, reqs)
    b_rows = jnp.concatenate([bc[0, pl.ds(first, reqs)], bc[1, pl.ds(first, reqs)]], axis=1)
    c_rows = jnp.concatenate([bc[2, pl.ds(first, reqs)], bc[3, pl.ds(first, reqs)]], axis=1)
    lane = lax.broadcasted_iota(jnp.int32, (chans, wide), 1)
    cols = [jnp.zeros((chans, wide), F32) for _ in range(heads)]
    for r in range(reqs):
        for h in range(heads):
            at = slice(h * chans, (h + 1) * chans)
            fresh = rt[at, r : r + 1] * state[r, h] + sx[at, r : r + 1] * b_rows[r : r + 1]
            new_state[r, h] = fresh
            out = jnp.sum(fresh * c_rows[r : r + 1], axis=1, keepdims=True)
            cols[h] = jnp.where(lane == r, out, cols[h])
    out = jnp.concatenate(cols, axis=0).T[:reqs]
    gated[...] = (out + skipx[...]) * gate[...]


def front_kernel(
    hid, wz, wx, wbc, wdt, *rest,
):
    smalls_in, rest = rest[:8], rest[8:]
    skipx, gate, sizex, retain, bc, cxn, cbn = rest[:7]
    blocks, xn, wz_v, wx_v, wbc_v, bc_own, bc_got = rest[7:14]
    smalls, rest = rest[14:22], rest[22:]
    wsem, bsem, hsem, ssem, ag_s, ag_r, bc_s, bc_r = rest
    gain, dtb, dec, skip, cxw, cbw, cxs, cbs = smalls
    me, z, x, c = coords()
    hid_cp = pltpu.make_async_copy(hid, blocks.at[me], hsem)
    hid_cp.start()
    small_cps = [
        pltpu.make_async_copy(smalls_in[i], smalls[i], ssem.at[i]) for i in range(len(smalls))
    ]
    for cp in small_cps:
        cp.start()
    rows = wx_v.shape[1]
    bc_cp = pltpu.make_async_copy(wbc, wbc_v, bsem)
    bc_cp.start()
    loads = []
    for i, (src, dst) in enumerate(((wx, wx_v), (wz, wz_v))):
        for k in range(4):
            cp = pltpu.make_async_copy(
                src.at[pl.ds(k * rows, rows), :], dst.at[k], wsem.at[i * 4 + k]
            )
            cp.start()
            loads.append(cp)
    greet(me)
    hid_cp.wait()
    started = gather_blocks(blocks, ag_s, ag_r)
    for cp in small_cps:
        cp.wait()
    norm_blocks(blocks, gain, xn)
    width = hid.shape[1]

    bc_cp.wait()
    acc = jnp.zeros(bc_own.shape, F32)
    for k in range(NDEV):
        acc += jnp.dot(xn[k], wbc_v[k * width : (k + 1) * width, :], preferred_element_type=F32)
    bc_own[...] = conv_rows(cbs, acc.astype(BF16), cbw, cbn).astype(BF16)
    goal, slot = (me % 8) // 2, (me // 8) * 2 + me % 2
    for i in range(4):
        dev = goal * 4 + i

        @pl.when(dev != me)
        def _():
            remote(bc_own, bc_got.at[slot], bc_s.at[i], bc_r.at[slot], dev).start()

        @pl.when(dev == me)
        def _():
            bc_got[slot] = bc_own[...]

    def project(w_v, first):
        acc = jnp.zeros(gate.shape, F32)
        for k in range(4):
            loads[first + k].wait()
            for j in range(4):
                acc += jnp.dot(
                    xn[k * 4 + j], w_v[k, j * width : (j + 1) * width, :],
                    preferred_element_type=F32,
                )
        return acc

    acc = jnp.zeros((hid.shape[0], dtb.shape[1]), F32)
    for k in range(NDEV):
        acc += lax.dot_general(
            xn[k], wdt[:, k * width : (k + 1) * width], (((1,), (1,)), ((), ())),
            preferred_element_type=F32,
        )
    raw = acc + dtb[...]
    size = jnp.maximum(raw, 0.0) + jnp.log1p(jnp.exp(-jnp.abs(raw)))
    retain[...] = per_channel(jnp.exp(-size * dec[...]), gate.shape)
    xv = conv_rows(cxs, project(wx_v, 0).astype(BF16), cxw, cxn)
    sizex[...] = per_channel(size, gate.shape) * xv
    skipx[...] = per_channel(jnp.broadcast_to(skip[...], size.shape), gate.shape) * xv
    zv = project(wz_v, 4)
    gate[...] = zv / (1.0 + jnp.exp(-zv))

    for i in range(4):
        src = (i // 2) * 8 + z * 2 + i % 2

        @pl.when(src != me)
        def _():
            remote(bc_own, bc_got.at[i], bc_s.at[0], bc_r.at[i], src).wait_recv()

    bc[...] = bc_got[...].astype(F32)
    for i in range(4):
        dev = goal * 4 + i

        @pl.when(dev != me)
        def _():
            remote(bc_own, bc_got.at[slot], bc_s.at[i], bc_r.at[slot], dev).wait_send()

    for cp in started:
        cp.wait_send()


def back_kernel(
    gated, ggain_in, hid_in, mgain_in, wo, wu, wd,
    result, ggain, hid, mgain,
    wo_v, wu_v, wd_v, y, act, parts, blocks, xn, sq_own, sq_got,
    csend, crecv, xsend, xrecv, zsend, zrecv,
    wsem, ssem, sq_s, sq_r, ag_s, ag_r, rs1, rs2,
):
    small_cps = [
        pltpu.make_async_copy(ggain_in, ggain, ssem.at[0]),
        pltpu.make_async_copy(hid_in, hid, ssem.at[1]),
        pltpu.make_async_copy(mgain_in, mgain, ssem.at[2]),
    ]
    for cp in small_cps:
        cp.start()
    me, z, x, c = coords()
    cols = wo_v.shape[2]
    rows = wu_v.shape[1]
    width = hid.shape[1]
    loads = {}
    for t in range(LINES):
        at = pl.multiple_of(((z + 1 + t) % LINES) * cols, cols)
        loads["o", t] = pltpu.make_async_copy(wo.at[:, pl.ds(at, cols)], wo_v.at[t], wsem.at[t])
    for t in range(LINES):
        loads["u", t] = pltpu.make_async_copy(
            wu.at[pl.ds(t * rows, rows), :], wu_v.at[t], wsem.at[4 + t]
        )
    for t in range(LINES):
        at = pl.multiple_of(((z + 1 + t) % LINES) * cols, cols)
        loads["d", t] = pltpu.make_async_copy(wd.at[:, pl.ds(at, cols)], wd_v.at[t], wsem.at[8 + t])
    for cp in loads.values():
        cp.start()
    g = gated[...]
    for cp in small_cps:
        cp.wait()
    y[...] = (g * ggain[...]).astype(BF16)
    sq_own[...] = jnp.broadcast_to(jnp.sum(g * g, axis=1, keepdims=True), sq_own.shape)
    greet(me)
    mates = (spot(z, x, 1 - c), spot(z, 1 - x, c), spot(z, 1 - x, 1 - c))
    sq_cp = [remote(sq_own, sq_got.at[i], sq_s.at[i], sq_r.at[i], mates[i]) for i in range(3)]
    for cp in sq_cp:
        cp.start()
    scale = []

    def group_scale(v):
        if not scale:
            total = sq_own[...]
            for i in range(3):
                sq_cp[i].wait_recv()
                total = total + sq_got[i]
            scale.append(lax.rsqrt(total[:, :1] / (4 * width) + 1e-05))
        return v * scale[0]

    def part(name, lhs, w_v):
        def fn(t, out):
            loads[name, t].wait()
            for b in range(4):
                out[t, b] = jnp.dot(
                    lhs[...], w_v[t, :, b * width : (b + 1) * width], preferred_element_type=F32
                )
        return fn

    mix, started = spread_sum(
        part("o", y, wo_v), group_scale, parts,
        csend.at[0], crecv.at[0], xsend.at[0], xrecv.at[0], zsend.at[0], zrecv.at[0],
        [rs1.at[i] for i in range(6)],
    )
    after = (hid[...].astype(F32) + mix).astype(BF16)
    blocks[me] = after
    started += sq_cp + gather_blocks(blocks, ag_s, ag_r)
    norm_blocks(blocks, mgain, xn)
    acc = jnp.zeros(act.shape, F32)
    for t in range(LINES):
        loads["u", t].wait()
        for j in range(4):
            acc += jnp.dot(
                xn[t * 4 + j], wu_v[t, j * width : (j + 1) * width, :], preferred_element_type=F32
            )
    act[...] = jnp.square(jnp.maximum(acc, 0.0)).astype(BF16)
    down, more = spread_sum(
        part("d", act, wd_v), lambda v: v, parts,
        csend.at[1], crecv.at[1], xsend.at[1], xrecv.at[1], zsend.at[1], zrecv.at[1],
        [rs2.at[i] for i in range(6)],
    )
    result[...] = (blocks[me].astype(F32) + down).astype(BF16)
    for cp in started + more:
        cp.wait_send()


def body(
    hidden, norm_in_gain, w_z, w_x, w_dt, w_bc, dt_bias, decay_rate, skip_gain,
    conv_x_weight, conv_bc_weight, conv_x_state, conv_bc_state, ssm_state,
    group_gain, w_out, norm_mid_gain, w_up, w_down,
):
    req, width = hidden.shape
    dim = w_x.shape[0]
    heads_dev = ssm_state.shape[1]
    inner = w_x.shape[1]
    bcw = w_bc.shape[1]
    ff = w_up.shape[1]
    dma = pltpu.SemaphoreType.DMA
    skipx, gate, sizex, retain, bc, cxn, cbn = pl.pallas_call(
        front_kernel,
        out_shape=[jax.ShapeDtypeStruct((req, inner), F32)] * 4
        + [
            jax.ShapeDtypeStruct((4, req, bcw), F32),
            jax.ShapeDtypeStruct((3, req, inner), BF16),
            jax.ShapeDtypeStruct((3, req, bcw), BF16),
        ],
        in_specs=[HB] * 4 + [VM] + [HB] * 8,
        out_specs=[VM] * 7,
        scratch_shapes=[
            pltpu.VMEM((NDEV, req, width), BF16),
            pltpu.VMEM((NDEV, req, width), BF16),
            pltpu.VMEM((4, dim // 4, inner), BF16),
            pltpu.VMEM((4, dim // 4, inner), BF16),
            pltpu.VMEM((dim, bcw), BF16),
            pltpu.VMEM((req, bcw), BF16),
            pltpu.VMEM((4, req, bcw), BF16),
            pltpu.VMEM((1, dim), F32),
            pltpu.VMEM((1, heads_dev), F32),
            pltpu.VMEM((1, heads_dev), F32),
            pltpu.VMEM((1, heads_dev), F32),
            pltpu.VMEM((4, inner), F32),
            pltpu.VMEM((4, bcw), F32),
            pltpu.VMEM((3, req, inner), BF16),
            pltpu.VMEM((3, req, bcw), BF16),
            dma((8,)), dma, dma, dma((8,)), dma((15,)), dma((16,)), dma((4,)), dma((4,)),
        ],
        compiler_params=pltpu.CompilerParams(
            collective_id=0, has_side_effects=True, vmem_limit_bytes=63 << 20
        ),
        name="front",
    )(
        hidden, w_z, w_x, w_bc, w_dt.T, norm_in_gain[None], dt_bias[None], decay_rate[None],
        skip_gain[None], conv_x_weight, conv_bc_weight,
        conv_x_state.transpose(1, 0, 2), conv_bc_state.transpose(1, 0, 2),
    )
    some = 8
    pair = 128 // HEAD_DIM
    chan = pl.BlockSpec((some, 128), lambda i, j: (i, j))
    held = pl.BlockSpec((some, pair, HEAD_DIM, N), lambda i, j: (i, j, 0, 0))
    whole = [
        pl.BlockSpec((4, req, bcw), lambda i, j: (0, 0, 0)),
        pl.BlockSpec((3, req, inner), lambda i, j: (0, 0, 0)),
        pl.BlockSpec((3, req, bcw), lambda i, j: (0, 0, 0)),
    ]
    ssm_new, gated, cxn, cbn = pl.pallas_call(
        state_kernel,
        grid=(req // some, heads_dev // pair),
        out_shape=[
            jax.ShapeDtypeStruct(ssm_state.shape, F32),
            jax.ShapeDtypeStruct((req, inner), F32),
            jax.ShapeDtypeStruct((3, req, inner), BF16),
            jax.ShapeDtypeStruct((3, req, bcw), BF16),
        ],
        in_specs=[held] + [chan] * 4 + whole,
        out_specs=[held, chan] + whole[1:],
        compiler_params=pltpu.CompilerParams(vmem_limit_bytes=63 << 20),
        name="state",
    )(ssm_state, sizex, retain, skipx, gate, bc, cxn, cbn)
    slot = (LINES, req, width)
    result = pl.pallas_call(
        back_kernel,
        out_shape=jax.ShapeDtypeStruct((req, width), BF16),
        in_specs=[VM] + [HB] * 6,
        out_specs=VM,
        scratch_shapes=[
            pltpu.VMEM((1, inner), F32),
            pltpu.VMEM((req, width), BF16),
            pltpu.VMEM((1, dim), F32),
            pltpu.VMEM((4, inner, dim // 4), BF16),
            pltpu.VMEM((4, dim // 4, ff), BF16),
            pltpu.VMEM((4, ff, dim // 4), BF16),
            pltpu.VMEM((req, inner), BF16),
            pltpu.VMEM((req, ff), BF16),
            pltpu.VMEM((4, 4, req, width), F32),
            pltpu.VMEM((NDEV, req, width), BF16),
            pltpu.VMEM((NDEV, req, width), BF16),
            pltpu.VMEM((req, 128), F32),
            pltpu.VMEM((3, req, 128), F32),
            pltpu.VMEM((2, 4, 2, req, width), BF16),
            pltpu.VMEM((2, 4, 2, req, width), BF16),
            pltpu.VMEM((2,) + slot, BF16),
            pltpu.VMEM((2,) + slot, BF16),
            pltpu.VMEM((2,) + slot, BF16),
            pltpu.VMEM((2,) + slot, BF16),
            dma((12,)), dma((3,)), dma((3,)), dma((3,)), dma((15,)), dma((16,)), dma((6, 4)), dma((6, 4)),
        ],
        compiler_params=pltpu.CompilerParams(
            collective_id=1, has_side_effects=True, vmem_limit_bytes=63 << 20
        ),
        name="back",
    )(gated, group_gain[None], hidden, norm_mid_gain[None], w_out, w_up, w_down)
    return (result, ssm_new, cxn.transpose(1, 0, 2), cbn.transpose(1, 0, 2))


def solution(mesh):
    in_specs = (
        P("groups", "gx"),
        P(),
        P(None, "gx"),
        P(None, "gx"),
        P(None, "gx"),
        P(None, "gx"),
        P("gx"),
        P("gx"),
        P("gx"),
        P(None, "gx"),
        P(None, "gx"),
        P("groups", None, "gx"),
        P("groups", None, "gx"),
        P("groups", "gx", None, None),
        P("gx"),
        P("gx", None),
        P(),
        P(None, "gx"),
        P("gx", None),
    )
    out_specs = (
        P("groups", "gx"),
        P("groups", "gx", None, None),
        P("groups", None, "gx"),
        P("groups", None, "gx"),
    )
    chosen = body if mesh.shape["gx"] == NDEV else plain_body
    return jax.shard_map(chosen, mesh=mesh, in_specs=in_specs, out_specs=out_specs, check_vma=False)
```

```python
import functools

import jax
import jax.numpy as jnp
from jax import lax
from jax.experimental import pallas as pl
from jax.experimental.pallas import tpu as pltpu
from jax.sharding import PartitionSpec as P

D = 8192
HEADS = 128
HEAD_DIM = 64
N = 256
G = 4
INNER = 8192


def rms_norm(values, gain_vec):
    inv_scale = lax.rsqrt(jnp.mean(values * values, axis=-1, keepdims=True) + 1e-05)
    return values * inv_scale * gain_vec


def conv_step(conv_state, fresh_cols, weight):
    window = jnp.concatenate([conv_state, fresh_cols[:, None, :]], axis=1)
    conv_sum = jnp.einsum(
        "rkc,kc->rc", window.astype(jnp.float32), weight, precision=lax.Precision.HIGHEST
    )
    return (jax.nn.silu(conv_sum), window[:, 1:])


def plain_body(
    hidden,
    norm_in_gain,
    w_z,
    w_x,
    w_dt,
    w_bc,
    dt_bias,
    decay_rate,
    skip_gain,
    conv_x_weight,
    conv_bc_weight,
    conv_x_state,
    conv_bc_state,
    ssm_state,
    group_gain,
    w_out,
    norm_mid_gain,
    w_up,
    w_down,
):
    position = lax.axis_index("gx")
    width_dev = hidden.shape[1]
    req_rows = hidden.shape[0]
    heads_dev = ssm_state.shape[1]
    full_rows = lax.all_gather(hidden, "gx", axis=1, tiled=True)
    normed = rms_norm(full_rows.astype(jnp.float32), norm_in_gain).astype(jnp.bfloat16)
    gate_z = jnp.dot(normed, w_z, preferred_element_type=jnp.float32)
    step_raw = jnp.dot(normed, w_dt, preferred_element_type=jnp.float32)
    x_raw = jnp.dot(normed, w_x, preferred_element_type=jnp.float32).astype(jnp.bfloat16)
    bc_raw = jnp.dot(normed, w_bc, preferred_element_type=jnp.float32).astype(jnp.bfloat16)
    x_conv, conv_x_new = conv_step(conv_x_state, x_raw, conv_x_weight)
    bc_conv, conv_bc_new = conv_step(conv_bc_state, bc_raw, conv_bc_weight)
    bc_full = lax.all_gather(bc_conv.astype(jnp.bfloat16), "gx", axis=1, tiled=True).astype(
        jnp.float32
    )
    group_idx = position * heads_dev // (HEADS // G)
    b_part = lax.dynamic_slice_in_dim(bc_full, group_idx * N, N, 1)
    c_part = lax.dynamic_slice_in_dim(bc_full, (G + group_idx) * N, N, 1)
    step_size = jax.nn.softplus(step_raw + dt_bias)
    retain = jnp.exp(-step_size * decay_rate)
    x_heads = x_conv.reshape(req_rows, heads_dev, HEAD_DIM)
    ssm_new = (
        retain[:, :, None, None] * ssm_state
        + (step_size[:, :, None] * x_heads)[..., None] * b_part[:, None, None, :]
    )
    head_out = (
        jnp.einsum("rhpn,rn->rhp", ssm_new, c_part, precision=lax.Precision.HIGHEST)
        + skip_gain[None, :, None] * x_heads
    )
    gated_out = head_out.reshape(req_rows, heads_dev * HEAD_DIM) * jax.nn.silu(gate_z)
    onehot = (jnp.arange(G) == group_idx).astype(jnp.float32)
    own_sq = jnp.sum(gated_out * gated_out, axis=-1)
    totals = lax.psum(own_sq[:, None] * onehot[None, :], "gx")
    mean_sq = jnp.sum(totals * onehot[None, :], axis=-1, keepdims=True) / (INNER // G)
    y_normed = (gated_out * lax.rsqrt(mean_sq + 1e-05) * group_gain).astype(jnp.bfloat16)
    mixer_terms = jnp.dot(y_normed, w_out, preferred_element_type=jnp.float32)
    mixer_out = lax.psum_scatter(mixer_terms, "gx", scatter_dimension=1, tiled=True)
    after_mix = (hidden.astype(jnp.float32) + mixer_out).astype(jnp.bfloat16)
    after_f = after_mix.astype(jnp.float32)
    total_sq = lax.psum(jnp.sum(after_f * after_f, axis=-1), "gx")
    gain_own = lax.dynamic_slice_in_dim(norm_mid_gain, position * width_dev, width_dev, 0)
    mid_own = (after_f * lax.rsqrt(total_sq[:, None] / D + 1e-05) * gain_own).astype(jnp.bfloat16)
    hidden_up = jnp.dot(
        lax.all_gather(mid_own, "gx", axis=1, tiled=True), w_up, preferred_element_type=jnp.float32
    )
    active = jnp.square(jnp.maximum(hidden_up, 0.0)).astype(jnp.bfloat16)
    down_sum = lax.psum_scatter(
        jnp.dot(active, w_down, preferred_element_type=jnp.float32),
        "gx",
        scatter_dimension=1,
        tiled=True,
    )
    result = (after_mix.astype(jnp.float32) + down_sum).astype(jnp.bfloat16)
    return (result, ssm_new, conv_x_new, conv_bc_new)


MESH = pl.DeviceIdType.MESH
NDEV = 16
LINES = 4
F32 = jnp.float32
BF16 = jnp.bfloat16
VM = pl.BlockSpec(memory_space=pltpu.VMEM)
HB = pl.BlockSpec(memory_space=pltpu.HBM)


def spot(z, x, c):
    return z * 4 + x * 2 + c


def coords():
    me = lax.axis_index("gx")
    return me, me // 4, (me // 2) % 2, me % 2


def remote(src, dst, send, recv, dev):
    return pltpu.make_async_remote_copy(
        src_ref=src, dst_ref=dst, send_sem=send, recv_sem=recv,
        device_id={"gx": dev}, device_id_type=MESH,
    )


def greet(me):
    barrier = pltpu.get_barrier_semaphore()
    for i in range(1, NDEV):
        pl.semaphore_signal(
            barrier, inc=1, device_id={"gx": (me + i) % NDEV}, device_id_type=MESH
        )
    pl.semaphore_wait(barrier, NDEV - 1)


def gather_blocks(blocks, send, recv):
    me, z, x, c = coords()
    started = []

    def put(b, dev):
        cp = remote(blocks.at[b], blocks.at[b], send.at[len(started)], recv.at[b], dev)
        cp.start()
        started.append(cp)

    def arrive(b):
        remote(blocks.at[b], blocks.at[b], send.at[0], recv.at[b], (me + 1) % NDEV).wait_recv()

    across, beside = spot(z, 1 - x, c), spot(z, x, 1 - c)
    for dz in (2, 1, 3):
        put(me, spot((z + dz) % LINES, x, c))
    put(me, across)
    put(me, beside)
    for dz in (1, 3, 2):
        b = spot((z + dz) % LINES, x, c)
        arrive(b)
        put(b, across)
        put(b, beside)
    for dz in (0, 1, 3, 2):
        b = spot((z + dz) % LINES, 1 - x, c)
        arrive(b)
        put(b, beside)
    for dz in (0, 1, 3, 2):
        arrive(spot((z + dz) % LINES, x, 1 - c))
        arrive(spot((z + dz) % LINES, 1 - x, 1 - c))
    return started


def norm_blocks(blocks, gain_ref, out):
    width = blocks.shape[2]
    total = jnp.zeros(blocks.shape[1:], F32)
    for k in range(NDEV):
        v = blocks[k].astype(F32)
        total += v * v
    inv = lax.rsqrt(jnp.sum(total, axis=1, keepdims=True) / (NDEV * width) + 1e-05)
    for k in range(NDEV):
        out[k] = (blocks[k].astype(F32) * inv * gain_ref[:, k * width : (k + 1) * width]).astype(BF16)


def spread_sum(part_fn, scale_fn, parts, csend, crecv, xsend, xrecv, zsend, zrecv, sems):
    me, z, x, c = coords()
    across, beside = spot(z, 1 - x, c), spot(z, x, 1 - c)
    cs, cr, xs, xr, zs, zr = sems
    ccp, xcp, zcp = {}, {}, {}
    own = None
    for step in range(LINES + 2):
        t = step
        if t < LINES:
            part_fn(t, parts)
            for xx in range(2):
                csend[t, xx] = parts[t, xx * 2 + (1 - c)].astype(BF16)
            ccp[t] = remote(csend.at[t], crecv.at[t], cs.at[t], cr.at[t], beside)
            ccp[t].start()
        t = step - 1
        if 0 <= t < LINES:
            ccp[t].wait_recv()
            xsend[t] = (parts[t, (1 - x) * 2 + c] + crecv[t, 1 - x].astype(F32)).astype(BF16)
            xcp[t] = remote(xsend.at[t], xrecv.at[t], xs.at[t], xr.at[t], across)
            xcp[t].start()
        t = step - 2
        if 0 <= t < LINES:
            xcp[t].wait_recv()
            v = parts[t, x * 2 + c] + crecv[t, x].astype(F32) + xrecv[t].astype(F32)
            v = scale_fn(v)
            if t < LINES - 1:
                zsend[t] = v.astype(BF16)
                zcp[t] = remote(
                    zsend.at[t], zrecv.at[t], zs.at[t], zr.at[t], spot((z + 1 + t) % LINES, x, c)
                )
                zcp[t].start()
            else:
                own = v
    for t in range(LINES - 1):
        zcp[t].wait_recv()
        own = own + zrecv[t].astype(F32)
    return own, list(ccp.values()) + list(xcp.values()) + list(zcp.values())


def conv_rows(state_ref, fresh, weight_ref, new_ref):
    total = fresh.astype(F32) * weight_ref[3:4, :]
    for k in range(3):
        total += state_ref[k].astype(F32) * weight_ref[k : k + 1, :]
    new_ref[0] = state_ref[1]
    new_ref[1] = state_ref[2]
    new_ref[2] = fresh
    return total / (1.0 + jnp.exp(-total))


def front_kernel(
    hid, wz, wx, wbc, wdt, *rest,
):
    smalls_in, rest = rest[:7], rest[7:]
    xconv, gate, step, retain, bc, cxn, cbn = rest[:7]
    blocks, xn, wz_v, wx_v, wbc_v, bc_own, bc_got = rest[7:14]
    smalls, rest = rest[14:21], rest[21:]
    wsem, bsem, hsem, ssem, ag_s, ag_r, bc_s, bc_r = rest
    gain, dtb, dec, cxw, cbw, cxs, cbs = smalls
    me, z, x, c = coords()
    hid_cp = pltpu.make_async_copy(hid, blocks.at[me], hsem)
    hid_cp.start()
    small_cps = [
        pltpu.make_async_copy(smalls_in[i], smalls[i], ssem.at[i]) for i in range(len(smalls))
    ]
    for cp in small_cps:
        cp.start()
    rows = wx_v.shape[1]
    bc_cp = pltpu.make_async_copy(wbc, wbc_v, bsem)
    bc_cp.start()
    loads = []
    for i, (src, dst) in enumerate(((wx, wx_v), (wz, wz_v))):
        for k in range(4):
            cp = pltpu.make_async_copy(
                src.at[pl.ds(k * rows, rows), :], dst.at[k], wsem.at[i * 4 + k]
            )
            cp.start()
            loads.append(cp)
    greet(me)
    hid_cp.wait()
    started = gather_blocks(blocks, ag_s, ag_r)
    for cp in small_cps:
        cp.wait()
    norm_blocks(blocks, gain, xn)
    width = hid.shape[1]

    bc_cp.wait()
    acc = jnp.zeros(bc_own.shape, F32)
    for k in range(NDEV):
        acc += jnp.dot(xn[k], wbc_v[k * width : (k + 1) * width, :], preferred_element_type=F32)
    bc_own[...] = conv_rows(cbs, acc.astype(BF16), cbw, cbn).astype(BF16)
    goal, slot = (me % 8) // 2, (me // 8) * 2 + me % 2
    for i in range(4):
        dev = goal * 4 + i

        @pl.when(dev != me)
        def _():
            remote(bc_own, bc_got.at[slot], bc_s.at[i], bc_r.at[slot], dev).start()

        @pl.when(dev == me)
        def _():
            bc_got[slot] = bc_own[...]

    def project(w_v, first):
        acc = jnp.zeros(gate.shape, F32)
        for k in range(4):
            loads[first + k].wait()
            for j in range(4):
                acc += jnp.dot(
                    xn[k * 4 + j], w_v[k, j * width : (j + 1) * width, :],
                    preferred_element_type=F32,
                )
        return acc

    acc = jnp.zeros((hid.shape[0], dtb.shape[1]), F32)
    for k in range(NDEV):
        acc += lax.dot_general(
            xn[k], wdt[:, k * width : (k + 1) * width], (((1,), (1,)), ((), ())),
            preferred_element_type=F32,
        )
    raw = acc + dtb[...]
    size = jnp.maximum(raw, 0.0) + jnp.log1p(jnp.exp(-jnp.abs(raw)))
    step[...] = size
    retain[...] = jnp.exp(-size * dec[...])
    xconv[...] = conv_rows(cxs, project(wx_v, 0).astype(BF16), cxw, cxn)
    zv = project(wz_v, 4)
    gate[...] = zv / (1.0 + jnp.exp(-zv))

    for i in range(4):
        src = (i // 2) * 8 + z * 2 + i % 2

        @pl.when(src != me)
        def _():
            remote(bc_own, bc_got.at[i], bc_s.at[0], bc_r.at[i], src).wait_recv()

    bc[...] = bc_got[...]
    for i in range(4):
        dev = goal * 4 + i

        @pl.when(dev != me)
        def _():
            remote(bc_own, bc_got.at[slot], bc_s.at[i], bc_r.at[slot], dev).wait_send()

    for cp in started:
        cp.wait_send()


def back_kernel(
    gated, ggain_in, hid_in, mgain_in, wo, wu, wd,
    result, ggain, hid, mgain,
    wo_v, wu_v, wd_v, y, act, parts, blocks, xn, sq_own, sq_got,
    csend, crecv, xsend, xrecv, zsend, zrecv,
    wsem, ssem, sq_s, sq_r, ag_s, ag_r, rs1, rs2,
):
    small_cps = [
        pltpu.make_async_copy(ggain_in, ggain, ssem.at[0]),
        pltpu.make_async_copy(hid_in, hid, ssem.at[1]),
        pltpu.make_async_copy(mgain_in, mgain, ssem.at[2]),
    ]
    for cp in small_cps:
        cp.start()
    me, z, x, c = coords()
    cols = wo_v.shape[2]
    rows = wu_v.shape[1]
    width = hid.shape[1]
    loads = {}
    for t in range(LINES):
        at = pl.multiple_of(((z + 1 + t) % LINES) * cols, cols)
        loads["o", t] = pltpu.make_async_copy(wo.at[:, pl.ds(at, cols)], wo_v.at[t], wsem.at[t])
    for t in range(LINES):
        loads["u", t] = pltpu.make_async_copy(
            wu.at[pl.ds(t * rows, rows), :], wu_v.at[t], wsem.at[4 + t]
        )
    for t in range(LINES):
        at = pl.multiple_of(((z + 1 + t) % LINES) * cols, cols)
        loads["d", t] = pltpu.make_async_copy(wd.at[:, pl.ds(at, cols)], wd_v.at[t], wsem.at[8 + t])
    for cp in loads.values():
        cp.start()
    g = gated[...]
    for cp in small_cps:
        cp.wait()
    y[...] = (g * ggain[...]).astype(BF16)
    sq_own[...] = jnp.broadcast_to(jnp.sum(g * g, axis=1, keepdims=True), sq_own.shape)
    greet(me)
    mates = (spot(z, x, 1 - c), spot(z, 1 - x, c), spot(z, 1 - x, 1 - c))
    sq_cp = [remote(sq_own, sq_got.at[i], sq_s.at[i], sq_r.at[i], mates[i]) for i in range(3)]
    for cp in sq_cp:
        cp.start()
    scale = []

    def group_scale(v):
        if not scale:
            total = sq_own[...]
            for i in range(3):
                sq_cp[i].wait_recv()
                total = total + sq_got[i]
            scale.append(lax.rsqrt(total[:, :1] / (4 * width) + 1e-05))
        return v * scale[0]

    def part(name, lhs, w_v):
        def fn(t, out):
            loads[name, t].wait()
            for b in range(4):
                out[t, b] = jnp.dot(
                    lhs[...], w_v[t, :, b * width : (b + 1) * width], preferred_element_type=F32
                )
        return fn

    mix, started = spread_sum(
        part("o", y, wo_v), group_scale, parts,
        csend.at[0], crecv.at[0], xsend.at[0], xrecv.at[0], zsend.at[0], zrecv.at[0],
        [rs1.at[i] for i in range(6)],
    )
    after = (hid[...].astype(F32) + mix).astype(BF16)
    blocks[me] = after
    started += sq_cp + gather_blocks(blocks, ag_s, ag_r)
    norm_blocks(blocks, mgain, xn)
    acc = jnp.zeros(act.shape, F32)
    for t in range(LINES):
        loads["u", t].wait()
        for j in range(4):
            acc += jnp.dot(
                xn[t * 4 + j], wu_v[t, j * width : (j + 1) * width, :], preferred_element_type=F32
            )
    act[...] = jnp.square(jnp.maximum(acc, 0.0)).astype(BF16)
    down, more = spread_sum(
        part("d", act, wd_v), lambda v: v, parts,
        csend.at[1], crecv.at[1], xsend.at[1], xrecv.at[1], zsend.at[1], zrecv.at[1],
        [rs2.at[i] for i in range(6)],
    )
    result[...] = (blocks[me].astype(F32) + down).astype(BF16)
    for cp in started + more:
        cp.wait_send()


def body(
    hidden, norm_in_gain, w_z, w_x, w_dt, w_bc, dt_bias, decay_rate, skip_gain,
    conv_x_weight, conv_bc_weight, conv_x_state, conv_bc_state, ssm_state,
    group_gain, w_out, norm_mid_gain, w_up, w_down,
):
    req, width = hidden.shape
    dim = w_x.shape[0]
    heads_dev = ssm_state.shape[1]
    inner = w_x.shape[1]
    bcw = w_bc.shape[1]
    ff = w_up.shape[1]
    dma = pltpu.SemaphoreType.DMA
    xconv, gate, step, retain, bc, cxn, cbn = pl.pallas_call(
        front_kernel,
        out_shape=[jax.ShapeDtypeStruct((req, inner), F32)] * 2
        + [jax.ShapeDtypeStruct((req, heads_dev), F32)] * 2
        + [
            jax.ShapeDtypeStruct((4, req, bcw), BF16),
            jax.ShapeDtypeStruct((3, req, inner), BF16),
            jax.ShapeDtypeStruct((3, req, bcw), BF16),
        ],
        in_specs=[HB] * 4 + [VM] + [HB] * 7,
        out_specs=[VM] * 7,
        scratch_shapes=[
            pltpu.VMEM((NDEV, req, width), BF16),
            pltpu.VMEM((NDEV, req, width), BF16),
            pltpu.VMEM((4, dim // 4, inner), BF16),
            pltpu.VMEM((4, dim // 4, inner), BF16),
            pltpu.VMEM((dim, bcw), BF16),
            pltpu.VMEM((req, bcw), BF16),
            pltpu.VMEM((4, req, bcw), BF16),
            pltpu.VMEM((1, dim), F32),
            pltpu.VMEM((1, heads_dev), F32),
            pltpu.VMEM((1, heads_dev), F32),
            pltpu.VMEM((4, inner), F32),
            pltpu.VMEM((4, bcw), F32),
            pltpu.VMEM((3, req, inner), BF16),
            pltpu.VMEM((3, req, bcw), BF16),
            dma((8,)), dma, dma, dma((7,)), dma((15,)), dma((16,)), dma((4,)), dma((4,)),
        ],
        compiler_params=pltpu.CompilerParams(
            collective_id=0, has_side_effects=True, vmem_limit_bytes=63 << 20
        ),
        name="front",
    )(
        hidden, w_z, w_x, w_bc, w_dt.T, norm_in_gain[None], dt_bias[None], decay_rate[None],
        conv_x_weight, conv_bc_weight,
        conv_x_state.transpose(1, 0, 2), conv_bc_state.transpose(1, 0, 2),
    )
    b_part = jnp.concatenate([bc[0], bc[1]], axis=1).astype(F32)
    c_part = jnp.concatenate([bc[2], bc[3]], axis=1).astype(F32)
    x_heads = xconv.reshape(req, heads_dev, HEAD_DIM)
    ssm_new = (
        retain[:, :, None, None] * ssm_state
        + (step[:, :, None] * x_heads)[..., None] * b_part[:, None, None, :]
    )
    head_out = (
        jnp.einsum("rhpn,rn->rhp", ssm_new, c_part, precision=lax.Precision.HIGHEST)
        + skip_gain[None, :, None] * x_heads
    )
    gated = head_out.reshape(req, inner) * gate
    slot = (LINES, req, width)
    result = pl.pallas_call(
        back_kernel,
        out_shape=jax.ShapeDtypeStruct((req, width), BF16),
        in_specs=[VM] + [HB] * 3 + [pl.BlockSpec(memory_space=pl.ANY)] * 3,
        out_specs=VM,
        scratch_shapes=[
            pltpu.VMEM((1, inner), F32),
            pltpu.VMEM((req, width), BF16),
            pltpu.VMEM((1, dim), F32),
            pltpu.VMEM((4, inner, dim // 4), BF16),
            pltpu.VMEM((4, dim // 4, ff), BF16),
            pltpu.VMEM((4, ff, dim // 4), BF16),
            pltpu.VMEM((req, inner), BF16),
            pltpu.VMEM((req, ff), BF16),
            pltpu.VMEM((4, 4, req, width), F32),
            pltpu.VMEM((NDEV, req, width), BF16),
            pltpu.VMEM((NDEV, req, width), BF16),
            pltpu.VMEM((req, 128), F32),
            pltpu.VMEM((3, req, 128), F32),
            pltpu.VMEM((2, 4, 2, req, width), BF16),
            pltpu.VMEM((2, 4, 2, req, width), BF16),
            pltpu.VMEM((2,) + slot, BF16),
            pltpu.VMEM((2,) + slot, BF16),
            pltpu.VMEM((2,) + slot, BF16),
            pltpu.VMEM((2,) + slot, BF16),
            dma((12,)), dma((3,)), dma((3,)), dma((3,)), dma((15,)), dma((16,)), dma((6, 4)), dma((6, 4)),
        ],
        compiler_params=pltpu.CompilerParams(
            collective_id=1, has_side_effects=True, vmem_limit_bytes=52 << 20
        ),
        name="back",
    )(gated, group_gain[None], hidden, norm_mid_gain[None], w_out, w_up, w_down)
    return (result, ssm_new, cxn.transpose(1, 0, 2), cbn.transpose(1, 0, 2))


def solution(mesh):
    in_specs = (
        P("groups", "gx"),
        P(),
        P(None, "gx"),
        P(None, "gx"),
        P(None, "gx"),
        P(None, "gx"),
        P("gx"),
        P("gx"),
        P("gx"),
        P(None, "gx"),
        P(None, "gx"),
        P("groups", None, "gx"),
        P("groups", None, "gx"),
        P("groups", "gx", None, None),
        P("gx"),
        P("gx", None),
        P(),
        P(None, "gx"),
        P("gx", None),
    )
    out_specs = (
        P("groups", "gx"),
        P("groups", "gx", None, None),
        P("groups", None, "gx"),
        P("groups", None, "gx"),
    )
    chosen = body if mesh.shape["gx"] == NDEV else plain_body
    return jax.shard_map(chosen, mesh=mesh, in_specs=in_specs, out_specs=out_specs, check_vma=False)
```
